256 devices in a mesh: fsdp: 64 (over z, x_hi, y), tensor: 4 (over x_lo, core).
Axes of the slice: x: 4 (x_hi: 2, x_lo: 2; x = x_hi * 2 + x_lo), y: 4, z: 8, core: 2. Of those that a mesh axis runs over, the one named last changes fastest.
Arguments:
- head_out: bfloat16 [32768, 3072], P('fsdp', 'tensor'), may hold values from -6 to 6
- stream: bfloat16 [32768, 4608], P('fsdp', 'tensor'), may hold values from -100 to 100
- tangent: bfloat16 [4608, 3072], P('fsdp', 'tensor'), may hold values from -2 to 2
- norm_gain: bfloat16 [4608], P('tensor'), may hold values from 0.099609375 to 1.8984375
- curvature: float32 [32768], P('fsdp'), may hold values from 0.001171875 to 0.01171875
- kept_counts: int32 [128], P('fsdp'), may hold values from 64 to 192, as said below
Outputs:
- curvature_product: float32 [4608, 3072], P('fsdp', 'tensor')
- normed_tangent: bfloat16 [32768, 4608], P('fsdp', 'tensor')
The draws below stay inside these ranges and needn't reach their ends.
Inputs may be any that keep to these rules, and one draw needn't show every extreme that they name: `kept_counts`: in every draw the 2 images of some index of fsdp each keep 192 patches.
All inputs are finite; a program needn't handle non-finite values.
Results may differ from the reference program's by a relative error of at most 0.015.
Values may be sent and summed in bfloat16 or wider, within the bound.
No kernel may reach another device: no remote copies, remote signals or barrier semaphores. Data moves between devices by JAX's collectives and lax.ppermute only.
A program may use at most 128 MiB of HBM per device.

```python
import math
import jax
import jax.numpy as jnp
from jax import lax

D = 4608
F = 3072
SLOTS = 256
KEEP_MOST = 192
KEEP_LEAST = 64
IMG_DEV = 2
IMAGES = 128
ROWS = 32768
N_TENSOR = 4


def shared_feature(key):
    return jnp.clip(jax.random.normal(jax.random.fold_in(key, 11), (D,)), -3.0, 3.0)


def draw_stream(key, part):
    feature = shared_feature(key)
    key = jax.random.fold_in(key, 5)
    first, second, third = jax.random.split(key, 3)
    row_scale = jnp.exp(jax.random.uniform(second, (ROWS, 1), minval=math.log(0.5), maxval=math.log(5.0)))
    col_scale = jnp.exp(jax.random.uniform(third, (1, D), minval=math.log(0.5), maxval=math.log(5.0)))
    base = jnp.clip(jax.random.normal(first, (ROWS, D)), -4.0, 4.0)
    mixed = (base + 0.6 * feature[None, :]) * row_scale * col_scale
    return jnp.clip(mixed, -100.0, 100.0).astype(jnp.bfloat16)


def draw_tangent(key, part):
    feature = shared_feature(key)
    key = jax.random.fold_in(key, 7)
    first, second = jax.random.split(key)
    noise = jnp.clip(jax.random.normal(first, (D, F)), -4.0, 4.0)
    across = jnp.clip(jax.random.normal(second, (F,)), -3.0, 3.0)
    return ((noise + feature[:, None] * across[None, :]) / math.sqrt(F)).astype(jnp.bfloat16)


def draw_kept_counts(key, part):
    key = jax.random.fold_in(key, 3)
    first, second = jax.random.split(key)
    counts = jax.random.randint(first, (IMAGES,), KEEP_LEAST, KEEP_MOST + 1)
    heavy = jax.random.randint(second, (), 0, IMAGES // IMG_DEV)
    owner = jnp.arange(IMAGES) // IMG_DEV
    return jnp.where(owner == heavy, KEEP_MOST, counts).astype(jnp.int32)


def block_levels(stream_key, dims, cuts, smallest, largest):
    def one(axis_at, shards_of):
        steps = jax.random.uniform(jax.random.fold_in(jax.random.fold_in(stream_key, 6), axis_at), (shards_of,), jnp.float32, smallest / len(cuts), largest / len(cuts))
        return jnp.repeat(jnp.exp(steps), dims[axis_at] // shards_of).reshape((-1,) + (1,) * (len(dims) - axis_at - 1))

    gain = one(*cuts[0])
    for cut in cuts[1:]:
        gain = gain * one(*cut)
    return gain


def normal_values(stream_key, extent, scale, reach, pieces=(), held_as=jnp.bfloat16):
    values = jax.random.normal(stream_key, extent, jnp.float32) * scale
    if len(pieces) > 0:
        values = block_levels(stream_key, extent, pieces, -0.22, 0.18) * values
    return jnp.clip(values, min=-reach, max=reach).astype(held_as)


def setup_inputs(seed: int = 0) -> dict:
    key_of = jax.random.split(jax.random.key(seed), 7)
    return {
        "head_out": normal_values(key_of[0], (ROWS, F), 1.0, 6.0, ((0, 64), (1, 4))),
        "stream": draw_stream(jax.random.fold_in(key_of[6], 71), 0),
        "tangent": draw_tangent(jax.random.fold_in(key_of[6], 71), 0),
        "norm_gain": jnp.clip(1.0 + 0.18 * jax.random.normal(key_of[3], (D,), jnp.float32), 0.099609375, 1.8984375).astype(jnp.bfloat16),
        "curvature": jnp.clip(jnp.exp(math.log(0.01171875) - 2.3025851 * jax.random.uniform(key_of[4], (ROWS,), jnp.float32) ** block_levels(key_of[4], (ROWS,), ((0, 64),), -0.2, 0.2)), 0.001171875, 0.01171875),
        "kept_counts": draw_kept_counts(jax.random.fold_in(key_of[6], 71), 0),
    }


EPS = 1e-06

def reference(head_out, stream, tangent, norm_gain, curvature, kept_counts):
    share = F // N_TENSOR
    live = (jnp.arange(SLOTS, dtype=jnp.int32)[None, :] < kept_counts[:, None]).astype(jnp.float32)
    complete_gain = norm_gain.astype(jnp.float32)[None, :]

    def one_image(total, items):
        block, hidden, weight, mask = items
        input_change = jnp.zeros((SLOTS, D), jnp.float32)
        for group in range(N_TENSOR):
            lower = group * share
            part = jnp.dot(block[:, lower:lower + share], tangent[:, lower:lower + share].T, preferred_element_type=jnp.float32)
            input_change = input_change + lax.optimization_barrier(part.astype(jnp.bfloat16)).astype(jnp.float32)
        values = hidden.astype(jnp.float32)
        centered_input = values - lax.optimization_barrier(jnp.mean(values, axis=1, keepdims=True))
        inverse_scale = lax.rsqrt(lax.optimization_barrier(jnp.mean(centered_input * centered_input, axis=1, keepdims=True)) + EPS)
        standardized_input = centered_input * inverse_scale
        normalized_input = complete_gain * (input_change - lax.optimization_barrier(jnp.mean(input_change, axis=1, keepdims=True)) - standardized_input * lax.optimization_barrier(jnp.mean(input_change * standardized_input, axis=1, keepdims=True))) * inverse_scale
        raised_output = complete_gain * (weight * mask)[:, None] * normalized_input
        backward_signal = ((raised_output - lax.optimization_barrier(jnp.mean(raised_output, axis=1, keepdims=True)) - standardized_input * lax.optimization_barrier(jnp.mean(raised_output * standardized_input, axis=1, keepdims=True))) * inverse_scale).astype(jnp.bfloat16)
        total = total + jnp.dot(backward_signal.T, block, preferred_element_type=jnp.float32)
        return (total, (normalized_input * mask[:, None]).astype(jnp.bfloat16))
    total, tangents = lax.scan(one_image, jnp.zeros((D, F), jnp.float32), (head_out.reshape(IMAGES, SLOTS, F), stream.reshape(IMAGES, SLOTS, D), curvature.reshape(IMAGES, SLOTS), live))
    return (total, tangents.reshape(IMAGES * SLOTS, D))
```

```python
import jax
import jax.numpy as jnp
import numpy as np
from jax import lax
from jax.sharding import Mesh
from jax.sharding import PartitionSpec as P

SLOTS = 256
KEEP_MOST = 192
EPS = 1e-06

SIZES = {"z": 8, "h": 2, "y": 4, "l": 2, "c": 2}
ALL = tuple(SIZES)
FSDP = ("z", "h", "y")
TENSOR = ("l", "c")
ACROSS = ("h", "l", "c")


def flat(z, h, y, t):
    return ((z * 2 + h) * 4 + y) * 4 + t


TO_GROUP = [
    (flat(z, h, y, t), flat(2 * t + h, z % 2, y, z // 2))
    for z in range(8)
    for h in range(2)
    for y in range(4)
    for t in range(4)
]
FROM_GROUP = [(b, a) for a, b in TO_GROUP]
SWAP = [(0, 1), (1, 0)]


def on_device(head_out, stream, tangent, norm_gain, curvature, kept_counts):
    images = kept_counts.shape[0]
    rows = images * KEEP_MOST
    features = head_out.shape[1]
    columns = stream.shape[1]
    half = columns // 2
    width = columns * 4
    height = tangent.shape[0]
    mine = lax.axis_index("h")

    live = lax.broadcasted_iota(jnp.int32, (images, SLOTS), 1) < kept_counts[:, None]
    weight = jnp.where(live, curvature.reshape(images, SLOTS), 0.0)[:, :KEEP_MOST].reshape(rows)
    head = head_out.reshape(images, SLOTS, features)[:, :KEEP_MOST].reshape(rows, features)
    hidden = stream.reshape(images, SLOTS, columns)[:, :KEEP_MOST].reshape(rows, columns)

    block = lax.ppermute(tangent, ALL, TO_GROUP)
    heads = lax.all_gather(head, ACROSS, axis=0)
    heads = heads.reshape(2, 4, rows, features)

    def by_h(own, other):
        pair = jnp.stack([own, other])
        return jnp.where(mine == 0, pair, pair[::-1])

    own_half = lax.dynamic_slice_in_dim(hidden, mine * half, half, 1)
    other_half = lax.dynamic_slice_in_dim(hidden, (1 - mine) * half, half, 1)
    values = by_h(own_half, lax.ppermute(other_half, "h", SWAP)).reshape(2 * rows, half)
    values = values.astype(jnp.float32)
    gain = lax.dynamic_slice_in_dim(norm_gain, mine * half, half, 0).astype(jnp.float32)[None, :]
    gain2 = gain * gain

    part_mean = jnp.mean(values, axis=1)
    part_square = jnp.mean(jnp.square(values - part_mean[:, None]), axis=1)
    stats = lax.all_gather(jnp.stack([part_mean, part_square]), ACROSS, axis=0)
    weights = lax.all_gather(weight, "h", axis=0).reshape(2 * rows)
    mean = jnp.mean(stats[:, 0], axis=0)
    square = jnp.mean(stats[:, 1] + jnp.square(stats[:, 0] - mean[None]), axis=0)
    scale = lax.rsqrt(square + EPS)
    xhat = (values - mean[:, None]) * scale[:, None]

    turned = lax.all_gather(lax.all_gather(block, "y", axis=0, tiled=True), "z", axis=0, tiled=True)
    turned = turned.reshape(4, half, features)
    change = jnp.concatenate(
        [
            sum(
                lax.dot_general(
                    heads[i, a],
                    turned[a],
                    (((1,), (1,)), ((), ())),
                    preferred_element_type=jnp.float32,
                )
                for a in range(4)
            )
            for i in range(2)
        ],
        axis=0,
    )
    raised = gain2 * change
    sums = jnp.stack(
        [
            jnp.sum(change, axis=1),
            jnp.sum(change * xhat, axis=1),
            jnp.sum(raised, axis=1),
            jnp.sum(raised * xhat, axis=1),
            jnp.sum(gain2 * xhat, axis=1),
            jnp.sum(gain2 * xhat * xhat, axis=1),
            jnp.broadcast_to(jnp.sum(gain2), (2 * rows,)),
        ]
    )
    sums = jnp.sum(lax.all_gather(sums, ACROSS, axis=0), axis=0) / width
    mean_change, mean_hat, mean_up, mean_up_hat, gain_hat, gain_hat2, gain_mean = sums
    first = weights * scale * (mean_up - mean_change * gain_mean - mean_hat * gain_hat)
    second = weights * scale * (mean_up_hat - mean_change * gain_hat - mean_hat * gain_hat2)
    normed = gain * (change - mean_change[:, None] - xhat * mean_hat[:, None]) * scale[:, None]
    lifted = gain * weights[:, None] * normed
    back = (lifted - first[:, None] - xhat * second[:, None]) * scale[:, None]
    back = back.astype(jnp.bfloat16).reshape(2, rows, half)

    partial = jnp.stack(
        [
            sum(
                lax.dot_general(
                    back[i],
                    heads[i, a],
                    (((0,), (0,)), ((), ())),
                    preferred_element_type=jnp.float32,
                )
                for i in range(2)
            ).astype(jnp.bfloat16)
            for a in range(4)
        ]
    )
    partial = partial.reshape(8, 4 * height, features)
    partial = lax.psum_scatter(partial, "z", scatter_dimension=0, tiled=True)
    partial = partial.reshape(4, height, features)
    partial = lax.psum_scatter(partial, "y", scatter_dimension=0, tiled=True)
    product = lax.ppermute(partial.reshape(height, features), ALL, FROM_GROUP).astype(jnp.float32)

    normed = normed.astype(jnp.bfloat16).reshape(2, rows, half)
    kept = lax.dynamic_index_in_dim(normed, mine, 0, keepdims=False)
    sent = lax.dynamic_index_in_dim(normed, 1 - mine, 0, keepdims=False)
    both = by_h(kept, lax.ppermute(sent, "h", SWAP))
    both = jnp.concatenate([both[0], both[1]], axis=1).reshape(images, KEEP_MOST, columns)
    both = jnp.where(live[:, :KEEP_MOST, None], both, 0).astype(jnp.bfloat16)
    both = jnp.pad(both, ((0, 0), (0, SLOTS - KEEP_MOST), (0, 0)))
    return product, both.reshape(images * SLOTS, columns)


def solution(mesh):
    fine = Mesh(mesh.devices.reshape(tuple(SIZES.values())), ALL)
    placed = (
        P(FSDP, TENSOR),
        P(FSDP, TENSOR),
        P(FSDP, TENSOR),
        P(TENSOR),
        P(FSDP),
        P(FSDP),
    )
    return jax.shard_map(
        on_device,
        mesh=fine,
        in_specs=placed,
        out_specs=(P(FSDP, TENSOR), P(FSDP, TENSOR)),
        check_vma=False,
    )
```

```python
import functools

import jax
import jax.numpy as jnp
from jax import lax
from jax.experimental import pallas as pl
from jax.experimental.pallas import tpu as pltpu
from jax.sharding import Mesh
from jax.sharding import PartitionSpec as P

SLOTS = 256
KEEP_MOST = 192
EPS = 1e-06

SIZES = {"z": 8, "h": 2, "y": 4, "l": 2, "c": 2}
ALL = tuple(SIZES)
FSDP = ("z", "h", "y")
TENSOR = ("l", "c")
XRING = ("h", "l")
LIMIT = 40 * 1024 * 1024


def flat(z, h, y, t):
    return ((z * 2 + h) * 4 + y) * 4 + t


THERE = [
    (flat(z, h, y, t), flat(2 * ((t + z // 2) % 4) + z % 2, h, y, z // 2))
    for z in range(8)
    for h in range(2)
    for y in range(4)
    for t in range(4)
]
BACK = [(b, a) for a, b in THERE]


def shift(x, axis, by):
    n = 4 if axis == XRING else SIZES[axis]
    return lax.ppermute(x, axis, [(i, (i + by) % n) for i in range(n)])


def after(first, *rest):
    return lax.optimization_barrier((first,) + rest)[1:]


def call(kernel, outs, flops, place, heads, *args):
    moved = sum(a.size * a.dtype.itemsize for a in heads + args)
    moved += sum(o.size * o.dtype.itemsize for o in outs)
    rows, features = heads[0].shape

    def body(place_ref, *refs):
        pieces, rest = refs[:8], refs[8:-2]
        whole, sems = refs[-2:]
        copies = [
            pltpu.make_async_copy(
                pieces[i], whole.at[i // 2, pl.ds((i % 2) * rows, rows)], sems.at[i]
            )
            for i in range(8)
        ]
        for copy in copies:
            copy.start()
        kernel(place_ref, (whole, copies), *rest)

    return pl.pallas_call(
        body,
        out_shape=outs,
        in_specs=[pl.BlockSpec(memory_space=pltpu.SMEM)]
        + [pl.BlockSpec(memory_space=pl.ANY)] * 8
        + [pl.BlockSpec(memory_space=pltpu.VMEM)] * len(args),
        out_specs=[pl.BlockSpec(memory_space=pltpu.VMEM)] * len(outs),
        scratch_shapes=[
            pltpu.VMEM((4, 2 * rows, features), jnp.bfloat16),
            pltpu.SemaphoreType.DMA((8,)),
        ],
        compiler_params=pltpu.CompilerParams(vmem_limit_bytes=LIMIT),
        cost_estimate=pl.CostEstimate(flops=flops, bytes_accessed=moved, transcendentals=0),
    )(place, *heads, *args)


def arrive(heads):
    whole, copies = heads
    for copy in copies:
        copy.wait()
    return whole


def group(place, offset):
    whose = lax.rem(lax.rem(place[0] + offset + 8, 8) // 2 - place[1] + 4, 4)
    return whose ^ place[1]


def add_pieces(offsets, place, heads, pieces, halves):
    for i, offset in enumerate(offsets):
        piece = jnp.concatenate([pieces[2 * i][...], pieces[2 * i + 1][...]], axis=0)
        term = lax.dot_general(
            piece,
            heads[group(place, offset)],
            (((1,), (1,)), ((), ())),
            preferred_element_type=jnp.float32,
        )
        k = offset % 2
        halves[k] = term if halves[k] is None else halves[k] + term
    return halves


def early_kernel(offsets, z_ref, heads, *refs):
    halves = add_pieces(offsets, z_ref, arrive(heads), refs[:-1], [None, None])
    refs[-1][0] = halves[0]
    refs[-1][1] = halves[1]


def late_kernel(offsets, z_ref, heads, early, xhat_ref, gain_ref, *refs):
    pieces, (change_ref, sums_ref) = refs[:-2], refs[-2:]
    halves = add_pieces(offsets, z_ref, arrive(heads), pieces, [early[0], early[1]])
    total = jnp.zeros((8, change_ref.shape[2]), jnp.float32)
    rows = []
    for k in range(2):
        change_ref[k] = halves[k]
        xhat = xhat_ref[k]
        gain = gain_ref[k]
        gain2 = gain * gain
        raised = gain2 * halves[k]
        lifted = gain2 * xhat
        parts = [
            halves[k],
            halves[k] * xhat,
            raised,
            raised * xhat,
            lifted,
            lifted * xhat,
            jnp.broadcast_to(gain2, xhat.shape),
        ]
        rows.append([jnp.sum(p, axis=0, keepdims=True) for p in parts])
    for i, (a, b) in enumerate(zip(*rows)):
        sums_ref[pl.ds(i, 1), :] = a + b
    sums_ref[pl.ds(7, 1), :] = total[:1]


def back_kernel(width, z_ref, heads, change_ref, xhat_ref, gain_ref, row_ref, *refs):
    sums, (back_ref, normed_ref), terms = refs[:4], refs[4:6], refs[6:]
    total = sum(s[...] for s in sums) * (1.0 / width)
    mean_change, mean_hat, mean_up, mean_up_hat, gain_hat, gain_hat2, gain_mean = (
        total[i : i + 1] for i in range(7)
    )
    weights, scale = row_ref[0:1, :], row_ref[1:2, :]
    factor = weights * scale
    first = factor * (mean_up - mean_change * gain_mean - mean_hat * gain_hat)
    second = factor * (mean_up_hat - mean_change * gain_hat - mean_hat * gain_hat2)
    for k in range(2):
        gain, xhat = gain_ref[k], xhat_ref[k]
        normed = gain * (change_ref[k] - mean_change - xhat * mean_hat) * scale
        normed_ref[k] = normed.astype(normed_ref.dtype)
        lifted = gain * weights * normed
        back_ref[k] = ((lifted - first - xhat * second) * scale).astype(back_ref.dtype)
    multiply((4, 3, -3), z_ref, arrive(heads), back_ref, terms)


def multiply(offsets, place, heads, back_ref, outs):
    for i, offset in enumerate(offsets):
        term = jnp.dot(
            back_ref[offset % 2], heads[group(place, offset)], preferred_element_type=jnp.float32
        )
        middle = term.shape[0] // 2
        outs[2 * i][...] = term[:middle].astype(outs[2 * i].dtype)
        outs[2 * i + 1][...] = term[middle:].astype(outs[2 * i + 1].dtype)


def terms_kernel(offsets, z_ref, heads, back_ref, *outs):
    multiply(offsets, z_ref, arrive(heads), back_ref, outs)


def on_device(head_out, stream, tangent, norm_gain, curvature, kept_counts):
    images = kept_counts.shape[0]
    rows = images * KEEP_MOST
    features = head_out.shape[1]
    columns = stream.shape[1]
    half = columns // 2
    quarter = half // 2
    height = tangent.shape[0]
    middle = 2 * height
    width = columns * 4
    z, h, y, l, c = (lax.axis_index(name) for name in ALL)
    odd = z % 2
    f32, bf16 = jnp.float32, jnp.bfloat16

    block = lax.ppermute(tangent, ALL, THERE)
    blocks = [block] + [shift(block, "y", by) for by in range(1, 4)]
    own = [jnp.concatenate(blocks[:2], axis=0), jnp.concatenate(blocks[2:], axis=0)]

    up, down = [list(own)], [list(own)]
    for step in range(1, 4):
        up.append([shift(x, "z", 1) for x in up[-1]])
        down.append([shift(x, "z", -1) for x in down[-1][::-1]][::-1])
    across = [shift(up[3][0], "z", 1), shift(down[3][1], "z", -1)]

    live = lax.broadcasted_iota(jnp.int32, (images, SLOTS), 1) < kept_counts[:, None]
    weight = jnp.where(live, curvature.reshape(images, SLOTS), 0.0)[:, :KEEP_MOST].reshape(rows)
    head = head_out.reshape(images, SLOTS, features)[:, :KEEP_MOST].reshape(rows, features)
    hidden = stream.reshape(images, SLOTS, columns)[:, :KEEP_MOST].reshape(rows, columns)

    chunks = hidden.T.reshape(2, 2, 4, height, rows)
    own_half = lax.dynamic_index_in_dim(chunks, h, 1, keepdims=False)
    other_half = lax.dynamic_index_in_dim(chunks, 1 - h, 1, keepdims=False)
    got_half = shift(other_half, "h", 1)

    def flip(x, axes, by):
        n = 4 if axes == XRING else 2
        return lax.ppermute(x, axes, [(i, i ^ by) for i in range(n)])

    (head,) = after(block, head)
    near = [head, *(flip(head, XRING, by) for by in (2, 1, 3))]
    beside = flip(head, "c", 1)
    near[1:] = after(up[2][1], *near[1:])
    far = [beside, *(flip(x, "c", 1) for x in near[1:])]
    heads = (near[0], near[1], far[0], far[1], near[2], near[3], far[2], far[3])

    def turned(x):
        x = jnp.where(odd == 0, x, x[::-1])
        x = [lax.dynamic_index_in_dim(x, (y - d) % 4, 1, keepdims=False) for d in range(4)]
        return jnp.concatenate(x, axis=1)

    (got_half,) = after(up[1][0], got_half)
    values = turned(jnp.concatenate([own_half, got_half], axis=-1)).astype(f32)
    gain = norm_gain.reshape(2, 2, 4, height).astype(f32)
    gain = turned(lax.dynamic_index_in_dim(gain, h, 1, keepdims=False)[..., None])

    part_mean = jnp.mean(values, axis=(0, 1))
    part_square = jnp.mean(jnp.square(values - part_mean), axis=(0, 1))
    def swapped(x):
        return jnp.concatenate([x[..., rows:], x[..., :rows]], axis=-1)

    def around(x):
        got = [flip(x, XRING, by) for by in (2, 1, 3)]
        return [x, swapped(got[0]), got[1], swapped(got[2])]

    stats = jnp.stack([part_mean, part_square, jnp.concatenate([weight, weight])])
    stats = jnp.stack([stats, flip(stats, "c", 1)])
    stats = around(stats)
    weights = jnp.concatenate([weight, stats[1][0, 2, rows:]])
    stats = jnp.concatenate(stats, axis=0)
    mean = jnp.mean(stats[:, 0], axis=0)
    square = jnp.mean(stats[:, 1] + jnp.square(stats[:, 0] - mean[None]), axis=0)
    scale = lax.rsqrt(square + EPS)
    xhat = (values - mean) * scale
    scalars = jnp.stack([weights, scale])

    place = jnp.stack([z, 2 * l + c]).astype(jnp.int32)
    shape = (2, quarter, 2 * rows)
    one = 2 * quarter * features * 2 * rows
    (early,) = call(
        functools.partial(early_kernel, (0, -1, 1, -2, 2)),
        [jax.ShapeDtypeStruct(shape, f32)],
        5 * one,
        place,
        heads,
        *own,
        *up[1],
        *down[1],
        *up[2],
        *down[2],
    )
    change, sums = call(
        functools.partial(late_kernel, (-3, 3, 4)),
        [jax.ShapeDtypeStruct(shape, f32), jax.ShapeDtypeStruct((8, 2 * rows), f32)],
        3 * one,
        place,
        heads,
        early,
        xhat,
        gain,
        *up[3],
        *down[3],
        *across,
    )
    sums = sums + flip(sums, "c", 1)
    half_shape = (middle, features)
    back, normed, *ready = call(
        functools.partial(back_kernel, width),
        [
            jax.ShapeDtypeStruct(shape, bf16),
            jax.ShapeDtypeStruct(shape, bf16),
            *[jax.ShapeDtypeStruct(half_shape, bf16)] * 2,
            *[jax.ShapeDtypeStruct(half_shape, f32)] * 4,
        ],
        3 * one,
        place,
        heads,
        change,
        xhat,
        gain,
        scalars,
        *around(sums),
    )

    first = {(1, 0): shift(ready[0], "z", 1), (-1, 1): shift(ready[1], "z", -1)}
    (held,) = after(first[1, 0], back)
    offsets = (2, -2, 1, -1, 0)
    terms = call(
        functools.partial(terms_kernel, offsets),
        [jax.ShapeDtypeStruct(half_shape, f32)] * 10,
        5 * one,
        place,
        heads,
        held,
    )
    ready = ready[2:] + list(terms)
    offsets = (3, -3) + offsets

    def term(offset, k):
        return ready[2 * offsets.index(offset) + k]

    total = []
    for k in range(2):
        sides = []
        for sign in (1, -1):
            run = term(3 * sign, k)
            if (sign, k) in first:
                run = run + first[sign, k].astype(f32)
            for step in (2, 1, 0):
                run = shift(run.astype(bf16), "z", sign).astype(f32)
                if step:
                    run = run + term(step * sign, k)
            sides.append(run)
        total.append(sides[0] + sides[1] + term(0, k))
    total = [t[i * height : (i + 1) * height] for t in total for i in range(2)]
    product = total[0] + sum(shift(total[d].astype(bf16), "y", -d).astype(f32) for d in range(1, 4))
    product = lax.ppermute(product.astype(bf16), ALL, BACK).astype(f32)

    normed = normed.reshape(2, 4, height, 2 * rows)
    normed = [lax.dynamic_index_in_dim(normed, (y - d) % 4, 1, keepdims=False) for d in range(4)]
    normed = jnp.stack(normed, axis=1)
    normed = jnp.where(odd == 0, normed, normed[::-1])
    kept, sent = normed[..., :rows], normed[..., rows:]
    got = shift(sent, "h", 1)
    both = jnp.stack([jnp.where(h == 0, kept, got), jnp.where(h == 0, got, kept)], axis=1)
    both = both.reshape(columns, rows).T
    both = both.reshape(images, KEEP_MOST, columns)
    both = jnp.where(live[:, :KEEP_MOST, None], both, 0).astype(bf16)
    both = jnp.pad(both, ((0, 0), (0, SLOTS - KEEP_MOST), (0, 0)))
    return product, both.reshape(images * SLOTS, columns)


def solution(mesh):
    fine = Mesh(mesh.devices.reshape(tuple(SIZES.values())), ALL)
    placed = (
        P(FSDP, TENSOR),
        P(FSDP, TENSOR),
        P(FSDP, TENSOR),
        P(TENSOR),
        P(FSDP),
        P(FSDP),
    )
    return jax.shard_map(
        on_device,
        mesh=fine,
        in_specs=placed,
        out_specs=(P(FSDP, TENSOR), P(FSDP, TENSOR)),
        check_vma=False,
    )
```

```python
import functools

import jax
import jax.numpy as jnp
from jax import lax
from jax.experimental import pallas as pl
from jax.experimental.pallas import tpu as pltpu
from jax.sharding import Mesh
from jax.sharding import PartitionSpec as P

SLOTS = 256
KEEP_MOST = 192
EPS = 1e-06

SIZES = {"z": 8, "h": 2, "y": 4, "l": 2, "c": 2}
ALL = tuple(SIZES)
FSDP = ("z", "h", "y")
TENSOR = ("l", "c")
XRING = ("h", "l")
LIMIT = 24 * 1024 * 1024


def flat(z, h, y, t):
    return ((z * 2 + h) * 4 + y) * 4 + t


THERE = [
    (flat(z, h, y, t), flat(2 * ((t + z // 2) % 4) + z % 2, h, y, z // 2))
    for z in range(8)
    for h in range(2)
    for y in range(4)
    for t in range(4)
]
BACK = [(b, a) for a, b in THERE]


def shift(x, axis, by):
    n = 4 if axis == XRING else SIZES[axis]
    return lax.ppermute(x, axis, [(i, (i + by) % n) for i in range(n)])


def after(first, *rest):
    return lax.optimization_barrier((first,) + rest)[1:]


def call(kernel, outs, flops, place, heads, *args):
    moved = sum(a.size * a.dtype.itemsize for a in (heads,) + args)
    moved += sum(o.size * o.dtype.itemsize for o in outs)
    _, rows, features = heads.shape

    def body(place_ref, *refs):
        pieces, rest = refs[0], refs[1:-2]
        whole, sems = refs[-2:]
        copies = [
            pltpu.make_async_copy(
                pieces.at[(i % 2 ^ place_ref[2]) * 4 + i // 2],
                whole.at[i // 2, pl.ds((i % 2) * rows, rows)],
                sems.at[i],
            )
            for i in range(8)
        ]
        for copy in copies:
            copy.start()
        kernel(place_ref, (whole, copies), *rest)

    return pl.pallas_call(
        body,
        out_shape=outs,
        in_specs=[pl.BlockSpec(memory_space=pltpu.SMEM)]
        + [pl.BlockSpec(memory_space=pl.ANY)]
        + [pl.BlockSpec(memory_space=pltpu.VMEM)] * len(args),
        out_specs=[pl.BlockSpec(memory_space=pltpu.VMEM)] * len(outs),
        scratch_shapes=[
            pltpu.VMEM((4, 2 * rows, features), jnp.bfloat16),
            pltpu.SemaphoreType.DMA((8,)),
        ],
        compiler_params=pltpu.CompilerParams(vmem_limit_bytes=LIMIT),
        cost_estimate=pl.CostEstimate(flops=flops, bytes_accessed=moved, transcendentals=0),
    )(place, heads, *args)


def arrive(heads):
    whole, copies = heads
    for copy in copies:
        copy.wait()
    return whole


def group(place, offset):
    return lax.rem(lax.rem(place[0] + offset + 8, 8) // 2 - place[1] + 4, 4)


def add_pieces(offsets, place, heads, pieces, halves):
    for i, offset in enumerate(offsets):
        piece = pieces[i][...]
        if offset == 4:
            piece = jnp.concatenate([piece, pieces[i + 1][...]], axis=0)
        term = lax.dot_general(
            piece,
            heads[group(place, offset)],
            (((1,), (1,)), ((), ())),
            preferred_element_type=jnp.float32,
        )
        k = offset % 2
        halves[k] = term if halves[k] is None else halves[k] + term
    return halves


def early_kernel(offsets, z_ref, heads, values_ref, own, far, near, beyond, *refs):
    pieces, (change_ref, xhat_ref, row_ref) = refs[:-3], refs[-3:]
    rows = own.shape[2] // 2

    def swapped(x):
        return jnp.concatenate([x[:, rows:], x[:, :rows]], axis=1)

    parts = [own[0], own[1], near[0], near[1]]
    parts += [swapped(x[i]) for x in (far, beyond) for i in range(2)]
    mean = sum(p[0:1] for p in parts) * 0.125
    square = sum(p[1:2] + jnp.square(p[0:1] - mean) for p in parts) * 0.125
    scale = lax.rsqrt(square + EPS)
    weights = jnp.concatenate([own[0][2:3, :rows], far[0][2:3, rows:]], axis=1)
    row_ref[...] = jnp.concatenate([weights, scale], axis=0)
    for k in range(2):
        xhat_ref[k] = (values_ref[k] - mean) * scale
    halves = add_pieces(offsets, z_ref, arrive(heads), pieces, [None, None])
    change_ref[0] = halves[0]
    change_ref[1] = halves[1]


def late_kernel(offsets, z_ref, heads, early, xhat_ref, gain_ref, *refs):
    pieces, (change_ref, sums_ref) = refs[:-2], refs[-2:]
    halves = add_pieces(offsets, z_ref, arrive(heads), pieces, [early[0], early[1]])
    total = jnp.zeros((8, change_ref.shape[2]), jnp.float32)
    rows = []
    for k in range(2):
        change_ref[k] = halves[k]
        xhat = xhat_ref[k]
        gain = gain_ref[k]
        gain2 = gain * gain
        raised = gain2 * halves[k]
        lifted = gain2 * xhat
        parts = [
            halves[k],
            halves[k] * xhat,
            raised,
            raised * xhat,
            lifted,
            lifted * xhat,
            jnp.broadcast_to(gain2, xhat.shape),
        ]
        rows.append([jnp.sum(p, axis=0, keepdims=True) for p in parts])
    for i, (a, b) in enumerate(zip(*rows)):
        sums_ref[pl.ds(i, 1), :] = a + b
    sums_ref[pl.ds(7, 1), :] = total[:1]


def back_kernel(width, z_ref, heads, change_ref, xhat_ref, gain_ref, row_ref, *refs):
    sums, (back_ref, normed_ref), terms = refs[:4], refs[4:6], refs[6:]
    total = sum(s[...] for s in sums) * (1.0 / width)
    mean_change, mean_hat, mean_up, mean_up_hat, gain_hat, gain_hat2, gain_mean = (
        total[i : i + 1] for i in range(7)
    )
    weights, scale = row_ref[0:1, :], row_ref[1:2, :]
    factor = weights * scale
    first = factor * (mean_up - mean_change * gain_mean - mean_hat * gain_hat)
    second = factor * (mean_up_hat - mean_change * gain_hat - mean_hat * gain_hat2)
    for k in range(2):
        gain, xhat = gain_ref[k], xhat_ref[k]
        normed = gain * (change_ref[k] - mean_change - xhat * mean_hat) * scale
        normed_ref[k] = normed.astype(normed_ref.dtype)
        lifted = gain * weights * normed
        back_ref[k] = ((lifted - first - xhat * second) * scale).astype(back_ref.dtype)
    multiply((4, 3, -3), z_ref, arrive(heads), back_ref, terms)


def multiply(offsets, place, heads, back_ref, outs):
    for i, offset in enumerate(offsets):
        term = jnp.dot(
            back_ref[offset % 2], heads[group(place, offset)], preferred_element_type=jnp.float32
        )
        if len(outs) == len(offsets):
            outs[i][...] = term
            continue
        middle = term.shape[0] // 2
        outs[2 * i][...] = term[:middle].astype(outs[2 * i].dtype)
        outs[2 * i + 1][...] = term[middle:].astype(outs[2 * i + 1].dtype)


def terms_kernel(offsets, z_ref, heads, back_ref, *outs):
    multiply(offsets, z_ref, arrive(heads), back_ref, outs)


def on_device(head_out, stream, tangent, norm_gain, curvature, kept_counts):
    images = kept_counts.shape[0]
    rows = images * KEEP_MOST
    features = head_out.shape[1]
    columns = stream.shape[1]
    half = columns // 2
    quarter = half // 2
    height = tangent.shape[0]
    middle = 2 * height
    width = columns * 4
    z, h, y, l, c = (lax.axis_index(name) for name in ALL)
    odd = z % 2
    f32, bf16 = jnp.float32, jnp.bfloat16

    live = lax.broadcasted_iota(jnp.int32, (images, SLOTS), 1) < kept_counts[:, None]
    weight = jnp.where(live, curvature.reshape(images, SLOTS), 0.0)[:, :KEEP_MOST].reshape(rows)
    head = head_out.reshape(images, SLOTS, features)[:, :KEEP_MOST].reshape(rows, features)
    hidden = stream.reshape(images, SLOTS, columns)[:, :KEEP_MOST].reshape(rows, columns)

    chunks = hidden.T.reshape(2, 2, 4, height, rows)
    own_half = lax.dynamic_index_in_dim(chunks, h, 1, keepdims=False)
    other_half = lax.dynamic_index_in_dim(chunks, 1 - h, 1, keepdims=False)

    block = lax.ppermute(tangent, ALL, THERE)
    block, own_half, other_half = lax.optimization_barrier((block, own_half, other_half))
    blocks = [block] + [shift(block, "y", by) for by in range(1, 4)]
    got_half = shift(other_half, "h", 1)
    *blocks, got_half = lax.optimization_barrier((*blocks, got_half))
    piece = jnp.concatenate(blocks, axis=0)
    (head,) = after(got_half, head)
    gathered = lax.all_gather(head, XRING + ("c",), axis=0)

    def flip(x, axes, by):
        n = 4 if axes == XRING else 2
        return lax.ppermute(x, axes, [(i, i ^ by) for i in range(n)])

    up, down = [piece], [piece]

    def step(*carried):
        ring = [shift(up[-1], "z", 1), shift(down[-1], "z", -1)]
        got = lax.optimization_barrier((*ring, *carried))
        up.append(got[0])
        down.append(got[1])
        return got[2:]

    step()

    def turned(x):
        x = jnp.where(odd == 0, x, x[::-1])
        x = [lax.dynamic_index_in_dim(x, (y - d) % 4, 1, keepdims=False) for d in range(4)]
        return jnp.concatenate(x, axis=1)

    values = turned(jnp.concatenate([own_half, got_half], axis=-1)).astype(f32)
    gain = norm_gain.reshape(2, 2, 4, height).astype(f32)
    gain = turned(lax.dynamic_index_in_dim(gain, h, 1, keepdims=False)[..., None])

    part_mean = jnp.mean(values, axis=(0, 1))
    part_square = jnp.mean(jnp.square(values - part_mean), axis=(0, 1))

    def swapped(x):
        return jnp.concatenate([x[..., rows:], x[..., :rows]], axis=-1)

    def around(x):
        got = [flip(x, XRING, by) for by in (2, 1, 3)]
        return [x, swapped(got[0]), got[1], swapped(got[2])]

    stats = jnp.stack([part_mean, part_square, jnp.concatenate([weight, weight])])
    (beside,) = step(flip(stats, "c", 1))
    stats = jnp.stack([stats, beside])
    x2, x1, x3 = step(*(flip(stats, XRING, by) for by in (2, 1, 3)))
    across = [shift(up[3][:middle], "z", 1), shift(down[3][middle:], "z", -1)]
    (gathered,) = after(up[2], gathered)
    place = jnp.stack([z, 2 * l + c, h]).astype(jnp.int32)
    shape = (2, quarter, 2 * rows)
    one = 2 * quarter * features * 2 * rows
    early, xhat, scalars = call(
        functools.partial(early_kernel, (0, -1, 1, -2, 2)),
        [
            jax.ShapeDtypeStruct(shape, f32),
            jax.ShapeDtypeStruct(shape, f32),
            jax.ShapeDtypeStruct((2, 2 * rows), f32),
        ],
        5 * one,
        place,
        gathered,
        values,
        stats,
        x2,
        x1,
        x3,
        piece,
        up[1],
        down[1],
        up[2],
        down[2],
    )
    change, sums = call(
        functools.partial(late_kernel, (-3, 3, 4)),
        [jax.ShapeDtypeStruct(shape, f32), jax.ShapeDtypeStruct((8, 2 * rows), f32)],
        3 * one,
        place,
        gathered,
        early,
        xhat,
        gain,
        up[3],
        down[3],
        *across,
    )
    sums = sums + flip(sums, "c", 1)
    half_shape = (middle, features)
    back, normed, *ready = call(
        functools.partial(back_kernel, width),
        [
            jax.ShapeDtypeStruct(shape, bf16),
            jax.ShapeDtypeStruct(shape, bf16),
            *[jax.ShapeDtypeStruct(half_shape, bf16)] * 2,
            *[jax.ShapeDtypeStruct(half_shape, f32)] * 4,
        ],
        3 * one,
        place,
        gathered,
        change,
        xhat,
        gain,
        scalars,
        *around(sums),
    )

    first = {(1, 0): shift(ready[0], "z", 1), (-1, 1): shift(ready[1], "z", -1)}
    (held,) = after(first[1, 0], back)
    offsets = (2, -2, 1, -1, 0)
    terms = call(
        functools.partial(terms_kernel, offsets),
        [jax.ShapeDtypeStruct((quarter, features), f32)] * 5,
        5 * one,
        place,
        gathered,
        held,
    )

    def term(offset, k=None):
        if k is None:
            return terms[offsets.index(offset)]
        return ready[2 * (3, -3).index(offset) + k + 2]

    up = jnp.concatenate([first[1, 0].astype(f32) + term(3, 0), term(3, 1)], axis=0)
    down = jnp.concatenate([term(-3, 0), first[-1, 1].astype(f32) + term(-3, 1)], axis=0)
    for step in (2, 1, 0):
        up = shift(up.astype(bf16), "z", 1).astype(f32)
        down = shift(down.astype(bf16), "z", -1).astype(f32)
        if step:
            up, down = up + term(step), down + term(-step)
    total = up + down + term(0)
    total = [total[i * height : (i + 1) * height] for i in range(4)]
    product = total[0] + sum(shift(total[d].astype(bf16), "y", -d).astype(f32) for d in range(1, 4))
    product = lax.ppermute(product.astype(bf16), ALL, BACK).astype(f32)

    normed = normed.reshape(2, 4, height, 2 * rows)
    normed = [lax.dynamic_index_in_dim(normed, (y - d) % 4, 1, keepdims=False) for d in range(4)]
    normed = jnp.stack(normed, axis=1)
    normed = jnp.where(odd == 0, normed, normed[::-1])
    kept, sent = normed[..., :rows], normed[..., rows:]
    got = shift(sent, "h", 1)
    both = jnp.stack([jnp.where(h == 0, kept, got), jnp.where(h == 0, got, kept)], axis=1)
    both = both.reshape(columns, rows).T
    both = both.reshape(images, KEEP_MOST, columns)
    both = jnp.where(live[:, :KEEP_MOST, None], both, 0).astype(bf16)
    both = jnp.pad(both, ((0, 0), (0, SLOTS - KEEP_MOST), (0, 0)))
    return product, both.reshape(images * SLOTS, columns)


def solution(mesh):
    fine = Mesh(mesh.devices.reshape(tuple(SIZES.values())), ALL)
    placed = (
        P(FSDP, TENSOR),
        P(FSDP, TENSOR),
        P(FSDP, TENSOR),
        P(TENSOR),
        P(FSDP),
        P(FSDP),
    )
    return jax.shard_map(
        on_device,
        mesh=fine,
        in_specs=placed,
        out_specs=(P(FSDP, TENSOR), P(FSDP, TENSOR)),
        check_vma=False,
    )
```

```python
import functools

import jax
import jax.numpy as jnp
from jax import lax
from jax.experimental import pallas as pl
from jax.experimental.pallas import tpu as pltpu
from jax.sharding import Mesh
from jax.sharding import PartitionSpec as P

SLOTS = 256
KEEP_MOST = 192
EPS = 1e-06

SIZES = {"z": 8, "h": 2, "y": 4, "l": 2, "c": 2}
ALL = tuple(SIZES)
FSDP = ("z", "h", "y")
TENSOR = ("l", "c")
XRING = ("h", "l")
LIMIT = 24 * 1024 * 1024


def flat(z, h, y, t):
    return ((z * 2 + h) * 4 + y) * 4 + t


THERE = [
    (flat(z, h, y, t), flat(2 * ((t + z // 2) % 4) + z % 2, h, y, z // 2))
    for z in range(8)
    for h in range(2)
    for y in range(4)
    for t in range(4)
]
BACK = [(b, a) for a, b in THERE]


def shift(x, axis, by):
    n = 4 if axis == XRING else SIZES[axis]
    return lax.ppermute(x, axis, [(i, (i + by) % n) for i in range(n)])


def after(first, *rest):
    return lax.optimization_barrier((first,) + rest)[1:]


def call(kernel, outs, flops, place, heads, *args):
    moved = sum(a.size * a.dtype.itemsize for a in (heads,) + args)
    moved += sum(o.size * o.dtype.itemsize for o in outs)
    _, rows, features = heads.shape

    def body(place_ref, *refs):
        pieces, rest = refs[0], refs[1:-2]
        whole, sems = refs[-2:]
        copies = [
            pltpu.make_async_copy(
                pieces.at[(i % 2 ^ place_ref[2]) * 4 + i // 2],
                whole.at[i // 2, pl.ds((i % 2) * rows, rows)],
                sems.at[i],
            )
            for i in range(8)
        ]
        for copy in copies:
            copy.start()
        kernel(place_ref, (whole, copies), *rest)

    return pl.pallas_call(
        body,
        out_shape=outs,
        in_specs=[pl.BlockSpec(memory_space=pltpu.SMEM)]
        + [pl.BlockSpec(memory_space=pl.ANY)]
        + [pl.BlockSpec(memory_space=pltpu.VMEM)] * len(args),
        out_specs=[pl.BlockSpec(memory_space=pltpu.VMEM)] * len(outs),
        scratch_shapes=[
            pltpu.VMEM((4, 2 * rows, features), jnp.bfloat16),
            pltpu.SemaphoreType.DMA((8,)),
        ],
        compiler_params=pltpu.CompilerParams(vmem_limit_bytes=LIMIT),
        cost_estimate=pl.CostEstimate(flops=flops, bytes_accessed=moved, transcendentals=0),
    )(place, heads, *args)


def arrive(heads):
    whole, copies = heads
    for copy in copies:
        copy.wait()
    return whole


def group(place, offset):
    return lax.rem(lax.rem(place[0] + offset + 8, 8) // 2 - place[1] + 4, 4)


def add_pieces(offsets, place, heads, pieces, halves):
    for i, offset in enumerate(offsets):
        piece = pieces[i][...]
        term = lax.dot_general(
            piece,
            heads[group(place, offset)],
            (((1,), (1,)), ((), ())),
            preferred_element_type=jnp.float32,
        )
        k = offset % 2
        halves[k] = term if halves[k] is None else halves[k] + term
    return halves


def early_kernel(offsets, z_ref, heads, values_ref, own, far, near, beyond, *refs):
    pieces, (change_ref, xhat_ref, row_ref) = refs[:-3], refs[-3:]
    rows = own.shape[2] // 2

    def swapped(x):
        return jnp.concatenate([x[:, rows:], x[:, :rows]], axis=1)

    parts = [own[0], own[1], near[0], near[1]]
    parts += [swapped(x[i]) for x in (far, beyond) for i in range(2)]
    mean = sum(p[0:1] for p in parts) * 0.125
    square = sum(p[1:2] + jnp.square(p[0:1] - mean) for p in parts) * 0.125
    scale = lax.rsqrt(square + EPS)
    weights = jnp.concatenate([own[0][2:3, :rows], far[0][2:3, rows:]], axis=1)
    row_ref[...] = jnp.concatenate([weights, scale], axis=0)
    for k in range(2):
        xhat_ref[k] = (values_ref[k] - mean) * scale
    halves = add_pieces(offsets, z_ref, arrive(heads), pieces, [None, None])
    change_ref[0] = halves[0]
    change_ref[1] = halves[1]


def late_kernel(offsets, z_ref, heads, early, xhat_ref, gain_ref, *refs):
    pieces, (change_ref, sums_ref) = refs[:-2], refs[-2:]
    halves = add_pieces(offsets, z_ref, arrive(heads), pieces, [early[0], early[1]])
    total = jnp.zeros((8, change_ref.shape[2]), jnp.float32)
    rows = []
    for k in range(2):
        change_ref[k] = halves[k]
        xhat = xhat_ref[k]
        gain = gain_ref[k]
        gain2 = gain * gain
        raised = gain2 * halves[k]
        lifted = gain2 * xhat
        parts = [
            halves[k],
            halves[k] * xhat,
            raised,
            raised * xhat,
            lifted,
            lifted * xhat,
            jnp.broadcast_to(gain2, xhat.shape),
        ]
        rows.append([jnp.sum(p, axis=0, keepdims=True) for p in parts])
    for i, (a, b) in enumerate(zip(*rows)):
        sums_ref[pl.ds(i, 1), :] = a + b
    sums_ref[pl.ds(7, 1), :] = total[:1]


def back_kernel(width, z_ref, heads, change_ref, xhat_ref, gain_ref, row_ref, *refs):
    sums, (back_ref, normed_ref), terms = refs[:4], refs[4:6], refs[6:]
    total = sum(s[...] for s in sums) * (1.0 / width)
    mean_change, mean_hat, mean_up, mean_up_hat, gain_hat, gain_hat2, gain_mean = (
        total[i : i + 1] for i in range(7)
    )
    weights, scale = row_ref[0:1, :], row_ref[1:2, :]
    factor = weights * scale
    first = factor * (mean_up - mean_change * gain_mean - mean_hat * gain_hat)
    second = factor * (mean_up_hat - mean_change * gain_hat - mean_hat * gain_hat2)
    for k in range(2):
        gain, xhat = gain_ref[k], xhat_ref[k]
        normed = gain * (change_ref[k] - mean_change - xhat * mean_hat) * scale
        normed_ref[k] = normed.astype(normed_ref.dtype)
        lifted = gain * weights * normed
        back_ref[k] = ((lifted - first - xhat * second) * scale).astype(back_ref.dtype)
    multiply((4, 3, -3), z_ref, arrive(heads), back_ref, terms)


def multiply(offsets, place, heads, back_ref, outs):
    for i, offset in enumerate(offsets):
        term = jnp.dot(
            back_ref[offset % 2], heads[group(place, offset)], preferred_element_type=jnp.float32
        )
        if len(outs) == len(offsets):
            outs[i][...] = term
            continue
        middle = term.shape[0] // 2
        outs[2 * i][...] = term[:middle].astype(outs[2 * i].dtype)
        outs[2 * i + 1][...] = term[middle:].astype(outs[2 * i + 1].dtype)


def terms_kernel(offsets, z_ref, heads, back_ref, *outs):
    multiply(offsets, z_ref, arrive(heads), back_ref, outs)


def on_device(head_out, stream, tangent, norm_gain, curvature, kept_counts):
    images = kept_counts.shape[0]
    rows = images * KEEP_MOST
    features = head_out.shape[1]
    columns = stream.shape[1]
    half = columns // 2
    quarter = half // 2
    height = tangent.shape[0]
    middle = 2 * height
    width = columns * 4
    z, h, y, l, c = (lax.axis_index(name) for name in ALL)
    odd = z % 2
    f32, bf16 = jnp.float32, jnp.bfloat16

    live = lax.broadcasted_iota(jnp.int32, (images, SLOTS), 1) < kept_counts[:, None]
    weight = jnp.where(live, curvature.reshape(images, SLOTS), 0.0)[:, :KEEP_MOST].reshape(rows)
    head = head_out.reshape(images, SLOTS, features)[:, :KEEP_MOST].reshape(rows, features)
    hidden = stream.reshape(images, SLOTS, columns)[:, :KEEP_MOST].reshape(rows, columns)

    chunks = hidden.T.reshape(2, 2, 4, height, rows)
    own_half = lax.dynamic_index_in_dim(chunks, h, 1, keepdims=False)
    other_half = lax.dynamic_index_in_dim(chunks, 1 - h, 1, keepdims=False)

    block = lax.ppermute(tangent, ALL, THERE)
    block, own_half, other_half = lax.optimization_barrier((block, own_half, other_half))
    blocks = [block] + [shift(block, "y", by) for by in range(1, 4)]
    got_half = shift(other_half, "h", 1)
    *blocks, got_half = lax.optimization_barrier((*blocks, got_half))
    piece = jnp.concatenate(blocks, axis=0)
    (head,) = after(got_half, head)
    gathered = lax.all_gather(head, XRING + ("c",), axis=0)

    def flip(x, axes, by):
        n = 4 if axes == XRING else 2
        return lax.ppermute(x, axes, [(i, i ^ by) for i in range(n)])

    up, down = [piece], [piece]

    def step(*carried):
        ring = [shift(up[-1], "z", 1), shift(down[-1], "z", -1)]
        got = lax.optimization_barrier((*ring, *carried))
        up.append(got[0])
        down.append(got[1])
        return got[2:]

    step()

    def turned(x):
        x = jnp.where(odd == 0, x, x[::-1])
        x = [lax.dynamic_index_in_dim(x, (y - d) % 4, 1, keepdims=False) for d in range(4)]
        return jnp.concatenate(x, axis=1)

    values = turned(jnp.concatenate([own_half, got_half], axis=-1)).astype(f32)
    gain = norm_gain.reshape(2, 2, 4, height).astype(f32)
    gain = turned(lax.dynamic_index_in_dim(gain, h, 1, keepdims=False)[..., None])

    part_mean = jnp.mean(values, axis=(0, 1))
    part_square = jnp.mean(jnp.square(values - part_mean), axis=(0, 1))

    def swapped(x):
        return jnp.concatenate([x[..., rows:], x[..., :rows]], axis=-1)

    def around(x):
        got = [flip(x, XRING, by) for by in (2, 1, 3)]
        return [x, swapped(got[0]), got[1], swapped(got[2])]

    stats = jnp.stack([part_mean, part_square, jnp.concatenate([weight, weight])])
    (beside,) = step(flip(stats, "c", 1))
    stats = jnp.stack([stats, beside])
    x2, x1, x3 = step(*(flip(stats, XRING, by) for by in (2, 1, 3)))
    across = [shift(up[3], "z", 1)]
    (gathered,) = after(up[2], gathered)
    place = jnp.stack([z, 2 * l + c, h]).astype(jnp.int32)
    shape = (2, quarter, 2 * rows)
    one = 2 * quarter * features * 2 * rows
    early, xhat, scalars = call(
        functools.partial(early_kernel, (0, -1, 1, -2, 2)),
        [
            jax.ShapeDtypeStruct(shape, f32),
            jax.ShapeDtypeStruct(shape, f32),
            jax.ShapeDtypeStruct((2, 2 * rows), f32),
        ],
        5 * one,
        place,
        gathered,
        values,
        stats,
        x2,
        x1,
        x3,
        piece,
        up[1],
        down[1],
        up[2],
        down[2],
    )
    change, sums = call(
        functools.partial(late_kernel, (-3, 3, 4)),
        [jax.ShapeDtypeStruct(shape, f32), jax.ShapeDtypeStruct((8, 2 * rows), f32)],
        3 * one,
        place,
        gathered,
        early,
        xhat,
        gain,
        up[3],
        down[3],
        *across,
    )
    sums = sums + flip(sums, "c", 1)
    half_shape = (middle, features)
    back, normed, *ready = call(
        functools.partial(back_kernel, width),
        [
            jax.ShapeDtypeStruct(shape, bf16),
            jax.ShapeDtypeStruct(shape, bf16),
            *[jax.ShapeDtypeStruct(half_shape, bf16)] * 2,
            *[jax.ShapeDtypeStruct(half_shape, f32)] * 4,
        ],
        3 * one,
        place,
        gathered,
        change,
        xhat,
        gain,
        scalars,
        *around(sums),
    )

    first = {(1, 0): shift(ready[0], "z", 1), (-1, 1): shift(ready[1], "z", -1)}
    (held,) = after(first[1, 0], back)
    offsets = (2, -2, 1, -1, 0)
    terms = call(
        functools.partial(terms_kernel, offsets),
        [jax.ShapeDtypeStruct((quarter, features), f32)] * 5,
        5 * one,
        place,
        gathered,
        held,
    )

    def term(offset, k=None):
        if k is None:
            return terms[offsets.index(offset)]
        return ready[2 * (3, -3).index(offset) + k + 2]

    up = jnp.concatenate([first[1, 0].astype(f32) + term(3, 0), term(3, 1)], axis=0)
    down = jnp.concatenate([term(-3, 0), first[-1, 1].astype(f32) + term(-3, 1)], axis=0)
    for step in (2, 1, 0):
        up = shift(up.astype(bf16), "z", 1).astype(f32)
        down = shift(down.astype(bf16), "z", -1).astype(f32)
        if step:
            up, down = up + term(step), down + term(-step)
    total = up + down + term(0)
    total = [total[i * height : (i + 1) * height] for i in range(4)]
    product = total[0] + sum(shift(total[d].astype(bf16), "y", -d).astype(f32) for d in range(1, 4))
    product = lax.ppermute(product.astype(bf16), ALL, BACK).astype(f32)

    normed = normed.reshape(2, 4, height, 2 * rows)
    normed = [lax.dynamic_index_in_dim(normed, (y - d) % 4, 1, keepdims=False) for d in range(4)]
    normed = jnp.stack(normed, axis=1)
    normed = jnp.where(odd == 0, normed, normed[::-1])
    kept, sent = normed[..., :rows], normed[..., rows:]
    got = shift(sent, "h", 1)
    both = jnp.stack([jnp.where(h == 0, kept, got), jnp.where(h == 0, got, kept)], axis=1)
    both = both.reshape(columns, rows).T
    both = both.reshape(images, KEEP_MOST, columns)
    both = jnp.where(live[:, :KEEP_MOST, None], both, 0).astype(bf16)
    both = jnp.pad(both, ((0, 0), (0, SLOTS - KEEP_MOST), (0, 0)))
    return product, both.reshape(images * SLOTS, columns)


def solution(mesh):
    fine = Mesh(mesh.devices.reshape(tuple(SIZES.values())), ALL)
    placed = (
        P(FSDP, TENSOR),
        P(FSDP, TENSOR),
        P(FSDP, TENSOR),
        P(TENSOR),
        P(FSDP),
        P(FSDP),
    )
    return jax.shard_map(
        on_device,
        mesh=fine,
        in_specs=placed,
        out_specs=(P(FSDP, TENSOR), P(FSDP, TENSOR)),
        check_vma=False,
    )
```
